32 devices in a mesh: groups: 2 (over y), tm: 4 (over z), weights: 2 (over core), batch: 2 (over x).
Axes of the slice: x: 2, y: 2, z: 4, core: 2. Of those that a mesh axis runs over, the one named last changes fastest.
Arguments:
- clip_feats: float32 [16, 8192, 128], P(('groups', 'weights', 'batch'), 'tm'), parts along dimension 0, may hold values from -6 to 6
- teacher: float32 [16, 4096, 256], P(('groups', 'weights', 'batch'), 'tm'), parts along dimension 0, may hold values from -6 to 6
- starts: int32 [16], P('groups'), parts along dimension 0, may hold values from 0 to 1023
- lengths: int32 [16], P('groups'), parts along dimension 0, may hold values from 2048 to 3072
- dilated_weight: float32 [7, 128, 128], replicated, may hold values from -0.1875 to 0.1875
- dilated_bias: float32 [128], replicated, may hold values from -0.5 to 0.5
- mix_w: float32 [128, 128], replicated, may hold values from -0.5 to 0.5
- mix_b: float32 [128], replicated, may hold values from -0.5 to 0.5
- down_w: float32 [4, 128, 256], replicated, may hold values from -0.25 to 0.25
- down_b: float32 [256], replicated, may hold values from -0.5 to 0.5
Outputs:
- grad_conv: float32 [14, 128, 128], P('groups', None, 'weights'), parts along dimension 0
- grad_conv_bias: float32 [256], P(('groups', 'weights')), parts along dimension 0
- grad_mix: float32 [256, 128], P(('groups', 'weights')), parts along dimension 0
- grad_mix_bias: float32 [256], P(('groups', 'weights')), parts along dimension 0
- grad_down: float32 [8, 128, 256], P('groups', None, 'weights'), parts along dimension 0
- grad_down_bias: float32 [512], P(('groups', 'weights')), parts along dimension 0
- loss: float32 [2], P('groups'), parts along dimension 0
The draws below stay inside these ranges and needn't reach their ends.
There are 2 independent parts, one for each index of `groups`. The reference program is written for one: setup_inputs(seed, part) draws one part's arguments, and reference() takes and returns one part's arrays. A program takes and returns all parts, laid end to end along the dimension named above; an argument that names none is the same for every part. Nothing has to cross between parts.
All inputs are finite; a program needn't handle non-finite values.
Results may differ from the reference program's by a relative error of at most 0.0003.
Values sent between devices are 32-bit elements; how exact they have to be, the bound alone decides.
A program may use at most 64 MiB of HBM per device.

```python
import jax
import jax.numpy as jnp
from jax import lax

C = 128
HID = 128
CO = 256
KERNEL_TAPS = 7
DILATION_RATE = 9
KDOWN = 4
INPUT_FRAMES = 8192
TO = 4096
BATCH = 8


def set_ends(values, key, least, high):
    dims = values.shape
    place = [jax.random.randint(jax.random.fold_in(key, axis), (), 0, dims[axis]) for axis in range(len(dims))]
    values = values.at[tuple(place)].set(least)
    longest = dims.index(max(dims))
    place[longest] = (place[longest] + 1) % dims[longest]
    return values.at[tuple(place)].set(high)


def block_levels(own_key, shape, pieces, smallest, largest):
    loudness, own = 1.0, jax.random.fold_in(own_key, 6)
    for axis_at, blocks in pieces:
        steps = jnp.exp(jax.random.uniform(jax.random.fold_in(own, axis_at), (blocks,), jnp.float32, smallest / len(pieces), largest / len(pieces)))
        loudness = loudness * jnp.repeat(steps, shape[axis_at] // blocks).reshape([-1 if axis == axis_at else 1 for axis in range(len(shape))])
    return loudness


def gaussian(stream_key, shape, width, limit, split=(), kind=jnp.bfloat16):
    values = width * jax.random.normal(stream_key, shape, jnp.float32)
    if split:
        values = values * block_levels(stream_key, shape, split, -0.22, 0.18)
    return jnp.clip(values, -limit, limit).astype(kind)


def setup_inputs(seed: int = 0, part: int = 0) -> dict:
    seeds = jax.random.split(jax.random.key(seed), 11)
    part_keys = jax.random.split(jax.random.fold_in(seeds[10], part), 11)
    return {
        "clip_feats": gaussian(part_keys[0], (BATCH, INPUT_FRAMES, C), 1.0, 6.0, ((0, 4), (1, 4)), jnp.float32),
        "teacher": gaussian(part_keys[1], (BATCH, TO, CO), 1.0, 6.0, ((0, 4), (1, 4)), jnp.float32),
        "starts": set_ends(jax.random.randint(part_keys[2], (BATCH,), 0, TO // 4), jax.random.fold_in(part_keys[2], 1), 0, (TO // 4) - 1).astype(jnp.int32),
        "lengths": set_ends(jax.random.randint(part_keys[3], (BATCH,), TO // 2, 3 * TO // 4 + 1), jax.random.fold_in(part_keys[3], 1), TO // 2, (3 * TO // 4 + 1) - 1).astype(jnp.int32),
        "dilated_weight": gaussian(seeds[4], (KERNEL_TAPS, C, HID), (KERNEL_TAPS * C) ** -0.5, 0.1875, (), jnp.float32),
        "dilated_bias": jnp.clip(jax.random.uniform(seeds[5], (HID,), jnp.float32, -0.5, 0.5), -0.5, 0.5),
        "mix_w": gaussian(seeds[6], (HID, C), HID ** -0.5, 0.5, (), jnp.float32),
        "mix_b": jnp.clip(jax.random.uniform(seeds[7], (C,), jnp.float32, -0.5, 0.5), -0.5, 0.5),
        "down_w": gaussian(seeds[8], (KDOWN, C, CO), (KDOWN * C) ** -0.5, 0.25, (), jnp.float32),
        "down_b": jnp.clip(jax.random.uniform(seeds[9], (CO,), jnp.float32, -0.5, 0.5), -0.5, 0.5),
    }


def elu_value(value):
    return jnp.where(value > 0, value, jnp.expm1(jnp.minimum(value, 0.0)))

def clip_error(params, features, target, valid_mask):
    dilated_weight, dilated_bias, mix_w, mix_b, down_w, down_b = params
    highest_precision = lax.Precision.HIGHEST
    receptive_reach = 3 * DILATION_RATE
    padded_input = jnp.pad(elu_value(features), ((receptive_reach, receptive_reach), (0, 0)))
    hidden_preactivation = dilated_bias + sum((jnp.dot(padded_input[DILATION_RATE * tap_index:DILATION_RATE * tap_index + INPUT_FRAMES], dilated_weight[tap_index], precision=highest_precision) for tap_index in range(KERNEL_TAPS)))
    section = features + jnp.dot(elu_value(hidden_preactivation), mix_w, precision=highest_precision) + mix_b
    framed = jnp.pad(elu_value(section), ((1, 1), (0, 0)))
    student = down_b + sum((jnp.dot(framed[tap_index:tap_index + 2 * TO:2], down_w[tap_index], precision=highest_precision) for tap_index in range(KDOWN)))
    error_term = student - target
    return jnp.sum(valid_mask[:, None] * error_term * error_term)

def reference(clip_feats, teacher, starts, lengths, dilated_weight, dilated_bias, mix_w, mix_b, down_w, down_b):
    params = (dilated_weight, dilated_bias, mix_w, mix_b, down_w, down_b)
    positions = jnp.arange(TO, dtype=jnp.int32)
    valid = ((positions[None, :] >= starts[:, None]) & (positions[None, :] < starts[:, None] + lengths[:, None])).astype(jnp.float32)
    scale = 1.0 / (jnp.sum(lengths).astype(jnp.float32) * CO)

    def one_clip(item):
        return jax.value_and_grad(clip_error)(params, item[0], item[1], item[2])
    errors, gradients = lax.map(one_clip, (clip_feats, teacher, valid))
    summed = [lax.optimization_barrier(jnp.sum(grad_item, axis=0)) * scale for grad_item in gradients]
    loss = (jnp.sum(errors) * scale).reshape(1)
    return (summed[0], summed[1], summed[2], summed[3], summed[4], summed[5], loss)
```

```python
import functools

import jax
import jax.numpy as jnp
from jax import lax
from jax.experimental import pallas as pl
from jax.experimental.pallas import tpu as pltpu
from jax.sharding import PartitionSpec as P

TAPS = 7
RATE = 9
HALO = 32
LEAD = 40
EDGE = 24
CHUNK = 256


def elu(v):
    return jnp.where(v > 0, v, jnp.exp(jnp.minimum(v, 0.0)) - 1.0)


def slope(e):
    return jnp.where(e > 0, 1.0, e + 1.0)


def mm(a, b):
    return lax.dot_general(a, b, (((1,), (0,)), ((), ())), precision=lax.Precision.HIGH,
                           preferred_element_type=jnp.float32)


def mm_t(a, b):
    return lax.dot_general(a, b, (((0,), (0,)), ((), ())), precision=lax.Precision.HIGH,
                           preferred_element_type=jnp.float32)


def local_kernel(
    bounds, x, xl, xr, te, tl, tr, wc, bc, wm, bm, wd, bd,
    o_conv, o_mix, o_down, o_bias,
    act, ya, yb, hid, sec, d0, d1, dsec, dhid, w2, wb, acc2, accd,
):
    step = pl.program_id(0)
    steps = pl.num_programs(0)
    T, C = x.shape[1], x.shape[2]
    N, CO = te.shape[1], te.shape[2]
    t0 = bounds[3] * T
    j0 = bounds[3] * N
    total = bounds[2] * T
    first = bounds[4 + 2 * step]
    last = first + bounds[5 + 2 * step]

    @pl.when(step == 0)
    def _():
        for k in range(TAPS + 1):
            m, p = k // 2, k % 2
            w2[m * C:(m + 1) * C, p * C:(p + 1) * C] = (
                wc[k] if k < TAPS else jnp.zeros((C, C), jnp.float32))
        for k in range(4):
            r, p = k // 2, k % 2
            wb[r * CO:(r + 1) * CO, p * C:(p + 1) * C] = wd[k].T
        acc2[...] = jnp.zeros_like(acc2)
        accd[...] = jnp.zeros_like(accd)
        o_mix[...] = jnp.zeros_like(o_mix)
        o_bias[...] = jnp.zeros_like(o_bias)
        dhid[...] = jnp.zeros_like(dhid)
        act[0:8] = jnp.zeros((8, C), jnp.float32)
        act[LEAD + T + HALO:] = jnp.zeros_like(act[LEAD + T + HALO:])
        sec[0:EDGE] = jnp.zeros((EDGE, C), jnp.float32)
        sec[EDGE + T + 8:] = jnp.zeros_like(sec[EDGE + T + 8:])

    act[8:LEAD] = elu(xl[0])
    act[LEAD + T:LEAD + T + HALO] = elu(xr[0])

    @pl.loop(0, T // CHUNK)
    def _(i):
        s = pl.multiple_of(i * CHUNK, CHUNK)
        act[pl.ds(LEAD + s, CHUNK)] = elu(x[0, pl.ds(s, CHUNK)])

    def conv(t, n):
        a = jnp.concatenate(
            [act[pl.ds(LEAD - 27 + 18 * m + t, n)] for m in range(4)], axis=1)
        r = mm(a, w2[...])
        row = pl.ds(8 + t, n)
        ya[row] = r[:, :C]
        yb[row] = r[:, C:]

    @pl.loop(0, T // CHUNK)
    def _(i):
        conv(i * CHUNK - 8, CHUNK)

    conv(T - 8, 32)

    def section(t, n, xv):
        h = ya[pl.ds(8 + t, n)] + yb[pl.ds(17 + t, n)] + bc[...]
        g = elu(h)
        hid[pl.ds(8 + t, n)] = g
        v = elu(xv + mm(g, wm[...]) + bm[...])
        pos = t0 + t + lax.broadcasted_iota(jnp.int32, (n, C), 0)
        sec[pl.ds(EDGE + t, n)] = jnp.where((pos >= 0) & (pos < total), v, 0.0)

    section(-8, 8, xl[0, HALO - 8:])
    section(T, 8, xr[0, :8])

    @pl.loop(0, T // CHUNK)
    def _(i):
        s = pl.multiple_of(i * CHUNK, CHUNK)
        section(s, CHUNK, x[0, pl.ds(s, CHUNK)])

    def error(j, n, tv):
        a = jnp.concatenate(
            [sec[pl.ds(EDGE + 2 * j + k - 1, n, stride=2)] for k in range(4)], axis=1)
        e = mm(a, wd[...].reshape(4 * C, CO)) + bd[...] - tv
        pos = j0 + j + lax.broadcasted_iota(jnp.int32, (n, CO), 0)
        d = jnp.where((pos >= first) & (pos < last), e, 0.0)
        d0[pl.ds(8 + j, n)] = d[:, :C]
        d1[pl.ds(8 + j, n)] = d[:, C:]
        return a, d

    error(-8, 8, tl[0])
    error(N, 8, tr[0])

    @pl.loop(0, N // CHUNK)
    def _(i):
        s = pl.multiple_of(i * CHUNK, CHUNK)
        a, d = error(s, CHUNK, te[0, pl.ds(s, CHUNK)])
        accd[...] += mm_t(a, d)
        o_bias[0:1, :] += jnp.sum(d, axis=0, keepdims=True)
        o_bias[1:2, :] += jnp.sum(d * d, axis=0, keepdims=True)

    def back(j, n):
        b = jnp.concatenate(
            [d0[pl.ds(8 + j, n)], d1[pl.ds(8 + j, n)],
             d0[pl.ds(7 + j, n)], d1[pl.ds(7 + j, n)]], axis=1)
        r = mm(b, wb[...])
        dsec[pl.ds(EDGE + 2 * j - 1, n, stride=2)] = r[:, :C]
        dsec[pl.ds(EDGE + 2 * j, n, stride=2)] = r[:, C:]

    @pl.loop(0, N // CHUNK)
    def _(i):
        back(pl.multiple_of(i * CHUNK, CHUNK), CHUNK)

    back(N, 8)

    @pl.loop(0, T // CHUNK)
    def _(i):
        s = pl.multiple_of(i * CHUNK, CHUNK)
        ds = dsec[pl.ds(EDGE + s, CHUNK)] * slope(sec[pl.ds(EDGE + s, CHUNK)])
        g = hid[pl.ds(8 + s, CHUNK)]
        o_mix[...] += mm_t(g, ds)
        dg = lax.dot_general(ds, wm[...], (((1,), (1,)), ((), ())),
                             precision=lax.Precision.HIGH,
                             preferred_element_type=jnp.float32)
        dh = dg * slope(g)
        dhid[pl.ds(16 + s, CHUNK)] = dh
        o_bias[2:3, :C] += jnp.sum(ds, axis=0, keepdims=True)
        o_bias[2:3, C:] += jnp.sum(dh, axis=0, keepdims=True)

    def taps(t, n):
        a = jnp.concatenate(
            [act[pl.ds(LEAD - 27 + 18 * m + t, n)] for m in range(4)], axis=1)
        d = jnp.concatenate(
            [dhid[pl.ds(16 + t, n)], dhid[pl.ds(7 + t, n)]], axis=1)
        acc2[...] += mm_t(a, d)

    @pl.loop(0, T // CHUNK)
    def _(i):
        taps(pl.multiple_of(i * CHUNK, CHUNK), CHUNK)

    taps(T, 16)

    @pl.when(step == steps - 1)
    def _():
        for k in range(TAPS):
            m, p = k // 2, k % 2
            o_conv[k] = acc2[m * C:(m + 1) * C, p * C:(p + 1) * C]
        for k in range(4):
            o_down[k] = accd[k * C:(k + 1) * C]


def local_grads(bounds, x, xl, xr, te, tl, tr, wc, bc, wm, bm, wd, bd):
    B, T, C = x.shape
    N, CO = te.shape[1:]
    f32 = jnp.float32

    def clip(a):
        return pl.BlockSpec((1,) + a.shape[1:], lambda i, *_: (i, 0, 0))

    def whole(a):
        return pl.BlockSpec(a.shape, lambda i, *_: (0,) * len(a.shape))

    outs = [jax.ShapeDtypeStruct(s, f32) for s in
            (wc.shape, wm.shape, wd.shape, (8, CO))]
    return pl.pallas_call(
        local_kernel,
        out_shape=outs,
        grid_spec=pltpu.PrefetchScalarGridSpec(
            num_scalar_prefetch=1,
            grid=(B,),
            in_specs=[clip(a) for a in (x, xl, xr, te, tl, tr)]
            + [whole(a) for a in (wc, bc, wm, bm, wd, bd)],
            out_specs=[whole(o) for o in outs],
            scratch_shapes=[
                pltpu.VMEM((LEAD + T + HALO + 56, C), f32),
                pltpu.VMEM((T + 32, C), f32),
                pltpu.VMEM((T + 32, C), f32),
                pltpu.VMEM((T + 16, C), f32),
                pltpu.VMEM((EDGE + T + 32, C), f32),
                pltpu.VMEM((N + 16, CO // 2), f32),
                pltpu.VMEM((N + 16, CO // 2), f32),
                pltpu.VMEM((EDGE + T + 32, C), f32),
                pltpu.VMEM((T + 32, C), f32),
                pltpu.VMEM((4 * C, 2 * C), f32),
                pltpu.VMEM((2 * CO, 2 * C), f32),
                pltpu.VMEM((4 * C, 2 * C), f32),
                pltpu.VMEM((4 * C, CO), f32),
            ],
        ),
        compiler_params=pltpu.CompilerParams(vmem_limit_bytes=48 * 2**20),
    )(bounds, x, xl, xr, te, tl, tr, wc, bc, wm, bm, wd, bd)


def shift(a, up):
    count = lax.axis_size("tm")
    pairs = [(i, i + 1) if up else (i + 1, i) for i in range(count - 1)]
    return lax.ppermute(a, "tm", pairs)


def shards(x, te, starts, lengths, wc, bc, wm, bm, wd, bd):
    B, T, C = x.shape
    N, CO = te.shape[1:]
    xl = shift(x[:, T - HALO:], True)
    xr = shift(x[:, :HALO], False)
    tl = shift(te[:, N - 8:], True)
    tr = shift(te[:, :8], False)
    mine = lax.axis_index(("weights", "batch")) * B
    own = jnp.stack([lax.dynamic_slice_in_dim(starts, mine, B),
                     lax.dynamic_slice_in_dim(lengths, mine, B)], axis=1).reshape(-1)
    tm = lax.axis_index("tm").astype(jnp.int32)
    head = jnp.stack([jnp.int32(0), jnp.int32(0), jnp.int32(lax.axis_size("tm")), tm])
    bounds = jnp.concatenate([head, own]).astype(jnp.int32)
    g_conv, g_mix, g_down, g_bias = local_grads(
        bounds, x, xl, xr, te, tl, tr, wc, bc.reshape(1, C), wm, bm.reshape(1, C),
        wd, bd.reshape(1, CO))
    g_conv, g_mix, g_down, g_bias = lax.psum(
        (g_conv, g_mix, g_down, g_bias), ("tm", "weights", "batch"))
    scale = 1.0 / (jnp.sum(lengths).astype(jnp.float32) * CO)
    two = 2.0 * scale
    p, n = lax.axis_index("weights"), lax.axis_size("weights")

    def panel(a, dim):
        w = a.shape[dim] // n
        return lax.dynamic_slice_in_dim(a, p * w, w, dim) * two

    return (
        panel(g_conv, 2),
        panel(g_bias[2, C:], 0),
        panel(g_mix, 0),
        panel(g_bias[2, :C], 0),
        panel(g_down, 2),
        panel(g_bias[0], 0),
        (jnp.sum(g_bias[1]) * scale).reshape(1),
    )


def solution(mesh):
    clips = P(("groups", "weights", "batch"), "tm", None)
    return jax.shard_map(
        shards,
        mesh=mesh,
        in_specs=(clips, clips, P("groups"), P("groups")) + (P(),) * 6,
        out_specs=(
            P("groups", None, "weights"),
            P(("groups", "weights")),
            P(("groups", "weights"), None),
            P(("groups", "weights")),
            P("groups", None, "weights"),
            P(("groups", "weights")),
            P("groups"),
        ),
        check_vma=False,
    )
```

```python
import functools

import jax
import jax.numpy as jnp
from jax import lax
from jax.experimental import pallas as pl
from jax.experimental.pallas import tpu as pltpu
from jax.sharding import PartitionSpec as P

TAPS = 7
RATE = 9
HALO = 32
LEAD = 40
EDGE = 24
CHUNK = 256


def elu(v):
    return jnp.where(v > 0, v, jnp.exp(jnp.minimum(v, 0.0)) - 1.0)


def slope(e):
    return jnp.where(e > 0, 1.0, e + 1.0)


def mm(a, b):
    return lax.dot_general(a, b, (((1,), (0,)), ((), ())), precision=lax.Precision.HIGH,
                           preferred_element_type=jnp.float32)


def mm_t(a, b):
    return lax.dot_general(a, b, (((0,), (0,)), ((), ())), precision=lax.Precision.HIGH,
                           preferred_element_type=jnp.float32)


def local_kernel(
    bounds, x, xl, xr, te, tl, tr, wc, bc, wm, bm, wd, bd,
    o_all,
    o_mix, o_bias, act, ya, yb, hid, sec, d0, d1, dsec, dhid, w2, wb, acc2, accd,
):
    step = pl.program_id(0)
    steps = pl.num_programs(0)
    T, C = x.shape[1], x.shape[2]
    N, CO = te.shape[1], te.shape[2]
    t0 = bounds[3] * T
    j0 = bounds[3] * N
    total = bounds[2] * T
    first = bounds[4 + 2 * step]
    last = first + bounds[5 + 2 * step]

    @pl.when(step == 0)
    def _():
        for k in range(TAPS + 1):
            m, p = k // 2, k % 2
            w2[m * C:(m + 1) * C, p * C:(p + 1) * C] = (
                wc[k] if k < TAPS else jnp.zeros((C, C), jnp.float32))
        for k in range(4):
            r, p = k // 2, k % 2
            wb[r * CO:(r + 1) * CO, p * C:(p + 1) * C] = wd[k].T
        acc2[...] = jnp.zeros_like(acc2)
        accd[...] = jnp.zeros_like(accd)
        o_mix[...] = jnp.zeros_like(o_mix)
        o_bias[...] = jnp.zeros_like(o_bias)
        dhid[...] = jnp.zeros_like(dhid)
        act[0:8] = jnp.zeros((8, C), jnp.float32)
        act[LEAD + T + HALO:] = jnp.zeros_like(act[LEAD + T + HALO:])
        sec[0:EDGE] = jnp.zeros((EDGE, C), jnp.float32)
        sec[EDGE + T + 8:] = jnp.zeros_like(sec[EDGE + T + 8:])

    act[8:LEAD] = elu(xl[0])
    act[LEAD + T:LEAD + T + HALO] = elu(xr[0])

    @pl.loop(0, T // CHUNK)
    def _(i):
        s = pl.multiple_of(i * CHUNK, CHUNK)
        act[pl.ds(LEAD + s, CHUNK)] = elu(x[0, pl.ds(s, CHUNK)])

    def conv(t, n):
        a = jnp.concatenate(
            [act[pl.ds(LEAD - 27 + 18 * m + t, n)] for m in range(4)], axis=1)
        r = mm(a, w2[...])
        row = pl.ds(8 + t, n)
        ya[row] = r[:, :C]
        yb[row] = r[:, C:]

    @pl.loop(0, T // CHUNK)
    def _(i):
        conv(i * CHUNK - 8, CHUNK)

    conv(T - 8, 32)

    def section(t, n, xv):
        h = ya[pl.ds(8 + t, n)] + yb[pl.ds(17 + t, n)] + bc[...]
        g = elu(h)
        hid[pl.ds(8 + t, n)] = g
        v = elu(xv + mm(g, wm[...]) + bm[...])
        pos = t0 + t + lax.broadcasted_iota(jnp.int32, (n, C), 0)
        sec[pl.ds(EDGE + t, n)] = jnp.where((pos >= 0) & (pos < total), v, 0.0)

    section(-8, 8, xl[0, HALO - 8:])
    section(T, 8, xr[0, :8])

    @pl.loop(0, T // CHUNK)
    def _(i):
        s = pl.multiple_of(i * CHUNK, CHUNK)
        section(s, CHUNK, x[0, pl.ds(s, CHUNK)])

    def error(j, n, tv):
        a = jnp.concatenate(
            [sec[pl.ds(EDGE + 2 * j + k - 1, n, stride=2)] for k in range(4)], axis=1)
        e = mm(a, wd[...].reshape(4 * C, CO)) + bd[...] - tv
        pos = j0 + j + lax.broadcasted_iota(jnp.int32, (n, CO), 0)
        d = jnp.where((pos >= first) & (pos < last), e, 0.0)
        d0[pl.ds(8 + j, n)] = d[:, :C]
        d1[pl.ds(8 + j, n)] = d[:, C:]
        return a, d

    error(-8, 8, tl[0])
    error(N, 8, tr[0])

    @pl.loop(0, N // CHUNK)
    def _(i):
        s = pl.multiple_of(i * CHUNK, CHUNK)
        a, d = error(s, CHUNK, te[0, pl.ds(s, CHUNK)])
        accd[...] += mm_t(a, d)
        o_bias[0:1, :] += jnp.sum(d, axis=0, keepdims=True)
        o_bias[1:2, :] += jnp.sum(d * d, axis=0, keepdims=True)

    def back(j, n):
        b = jnp.concatenate(
            [d0[pl.ds(8 + j, n)], d1[pl.ds(8 + j, n)],
             d0[pl.ds(7 + j, n)], d1[pl.ds(7 + j, n)]], axis=1)
        r = mm(b, wb[...])
        dsec[pl.ds(EDGE + 2 * j - 1, n, stride=2)] = r[:, :C]
        dsec[pl.ds(EDGE + 2 * j, n, stride=2)] = r[:, C:]

    @pl.loop(0, N // CHUNK)
    def _(i):
        back(pl.multiple_of(i * CHUNK, CHUNK), CHUNK)

    back(N, 8)

    @pl.loop(0, T // CHUNK)
    def _(i):
        s = pl.multiple_of(i * CHUNK, CHUNK)
        ds = dsec[pl.ds(EDGE + s, CHUNK)] * slope(sec[pl.ds(EDGE + s, CHUNK)])
        g = hid[pl.ds(8 + s, CHUNK)]
        o_mix[...] += mm_t(g, ds)
        dg = lax.dot_general(ds, wm[...], (((1,), (1,)), ((), ())),
                             precision=lax.Precision.HIGH,
                             preferred_element_type=jnp.float32)
        dh = dg * slope(g)
        dhid[pl.ds(16 + s, CHUNK)] = dh
        o_bias[2:3, :C] += jnp.sum(ds, axis=0, keepdims=True)
        o_bias[2:3, C:] += jnp.sum(dh, axis=0, keepdims=True)

    def taps(t, n):
        a = jnp.concatenate(
            [act[pl.ds(LEAD - 27 + 18 * m + t, n)] for m in range(4)], axis=1)
        d = jnp.concatenate(
            [dhid[pl.ds(16 + t, n)], dhid[pl.ds(7 + t, n)]], axis=1)
        acc2[...] += mm_t(a, d)

    @pl.loop(0, T // CHUNK)
    def _(i):
        taps(pl.multiple_of(i * CHUNK, CHUNK), CHUNK)

    taps(T, 16)

    @pl.when(step == steps - 1)
    def _():
        h = C // 2
        for p in range(2):
            c = slice(p * h, (p + 1) * h)
            d = slice(C + p * h, C + (p + 1) * h)
            o_all[p, 0:4 * C, :h] = acc2[:, c]
            o_all[p, 0:3 * C, h:] = acc2[0:3 * C, d]
            o_all[p, 3 * C:3 * C + h, h:] = o_mix[c, :h]
            o_all[p, 3 * C + h:4 * C, h:] = o_mix[c, h:]
            o_all[p, 4 * C:8 * C] = accd[:, p * C:(p + 1) * C]
            o_all[p, 8 * C:] = jnp.zeros_like(o_all[p, 8 * C:])
            o_all[p, 8 * C:8 * C + 1] = o_bias[0:1, p * C:(p + 1) * C]
            o_all[p, 8 * C + 1:8 * C + 2, :h] = o_bias[2:3, c]
            o_all[p, 8 * C + 1:8 * C + 2, h:] = o_bias[2:3, d]
            o_all[p, 8 * C + 2:8 * C + 3] = o_bias[1:2, :C] + o_bias[1:2, C:]


def local_grads(rows, bounds, x, xl, xr, te, tl, tr, wc, bc, wm, bm, wd, bd):
    B, T, C = x.shape
    N, CO = te.shape[1:]
    f32 = jnp.float32

    def clip(a):
        return pl.BlockSpec((1,) + a.shape[1:], lambda i, *_: (i, 0, 0))

    def whole(a):
        return pl.BlockSpec(a.shape, lambda i, *_: (0,) * len(a.shape))

    out = jax.ShapeDtypeStruct((2, rows, C), f32)
    return pl.pallas_call(
        local_kernel,
        out_shape=out,
        grid_spec=pltpu.PrefetchScalarGridSpec(
            num_scalar_prefetch=1,
            grid=(B,),
            in_specs=[clip(a) for a in (x, xl, xr, te, tl, tr)]
            + [whole(a) for a in (wc, bc, wm, bm, wd, bd)],
            out_specs=whole(out),
            scratch_shapes=[
                pltpu.VMEM((C, C), f32),
                pltpu.VMEM((8, CO), f32),
                pltpu.VMEM((LEAD + T + HALO + 56, C), f32),
                pltpu.VMEM((T + 32, C), f32),
                pltpu.VMEM((T + 32, C), f32),
                pltpu.VMEM((T + 16, C), f32),
                pltpu.VMEM((EDGE + T + 32, C), f32),
                pltpu.VMEM((N + 16, CO // 2), f32),
                pltpu.VMEM((N + 16, CO // 2), f32),
                pltpu.VMEM((EDGE + T + 32, C), f32),
                pltpu.VMEM((T + 32, C), f32),
                pltpu.VMEM((4 * C, 2 * C), f32),
                pltpu.VMEM((2 * CO, 2 * C), f32),
                pltpu.VMEM((4 * C, 2 * C), f32),
                pltpu.VMEM((4 * C, CO), f32),
            ],
        ),
        compiler_params=pltpu.CompilerParams(vmem_limit_bytes=48 * 2**20),
    )(bounds, x, xl, xr, te, tl, tr, wc, bc, wm, bm, wd, bd)


def halo_kernel(x, te, xl, xr, tl, tr, sxl, sxr, stl, str_, send, recv):
    count = lax.axis_size("tm")
    tm = lax.axis_index("tm")
    T, N = x.shape[1], te.shape[1]
    has_left, has_right = tm > 0, tm < count - 1
    barrier = pltpu.get_barrier_semaphore()

    def copy(k, src, dst, to):
        return pltpu.make_async_remote_copy(
            src_ref=src, dst_ref=dst, send_sem=send.at[k], recv_sem=recv.at[k],
            device_id={"tm": to}, device_id_type=pl.DeviceIdType.MESH)

    up = [copy(0, x.at[:, pl.ds(T - HALO, HALO)], sxl, tm + 1),
          copy(1, te.at[:, pl.ds(N - 8, 8)], stl, tm + 1)]
    down = [copy(2, x.at[:, pl.ds(0, HALO)], sxr, tm - 1),
            copy(3, te.at[:, pl.ds(0, 8)], str_, tm - 1)]

    @pl.when(has_left)
    def _():
        pl.semaphore_signal(barrier, inc=1, device_id={"tm": tm - 1},
                            device_id_type=pl.DeviceIdType.MESH)

    @pl.when(has_right)
    def _():
        pl.semaphore_signal(barrier, inc=1, device_id={"tm": tm + 1},
                            device_id_type=pl.DeviceIdType.MESH)

    pl.semaphore_wait(barrier, has_left.astype(jnp.int32) + has_right.astype(jnp.int32))

    @pl.when(has_right)
    def _():
        for c in up:
            c.start()

    @pl.when(has_left)
    def _():
        for c in down:
            c.start()

    @pl.when(has_left)
    def _():
        for c in up:
            c.wait_recv()
        xl[...] = sxl[...]
        tl[...] = stl[...]

    @pl.when(tm == 0)
    def _():
        xl[...] = jnp.zeros_like(xl)
        tl[...] = jnp.zeros_like(tl)

    @pl.when(has_right)
    def _():
        for c in down:
            c.wait_recv()
        xr[...] = sxr[...]
        tr[...] = str_[...]

    @pl.when(tm == count - 1)
    def _():
        xr[...] = jnp.zeros_like(xr)
        tr[...] = jnp.zeros_like(tr)

    @pl.when(has_right)
    def _():
        for c in up:
            c.wait_send()

    @pl.when(has_left)
    def _():
        for c in down:
            c.wait_send()


def halos(x, te):
    B, T, C = x.shape
    CO = te.shape[2]
    shapes = [(B, HALO, C), (B, HALO, C), (B, 8, CO), (B, 8, CO)]
    return pl.pallas_call(
        halo_kernel,
        out_shape=[jax.ShapeDtypeStruct(s, jnp.float32) for s in shapes],
        in_specs=[pl.BlockSpec(memory_space=pl.ANY)] * 2,
        out_specs=[pl.BlockSpec(memory_space=pltpu.VMEM)] * 4,
        scratch_shapes=[pltpu.VMEM(s, jnp.float32) for s in shapes]
        + [pltpu.SemaphoreType.DMA((4,)), pltpu.SemaphoreType.DMA((4,))],
        compiler_params=pltpu.CompilerParams(
            collective_id=0, has_side_effects=True, vmem_limit_bytes=16 * 2**20),
    )(x, te)


def reduce_kernel(parts, full, near, total, slots, sem, send, recv, send2, recv2):
    p = lax.axis_index("weights")
    nb, n = lax.axis_size("batch"), lax.axis_size("batch") * lax.axis_size("tm")
    me = lax.axis_index("tm") * nb + lax.axis_index("batch")
    chunk = full.shape[0] // n

    def place(d):
        r = lax.rem(me + d, n)
        return r, {"tm": r // nb, "batch": lax.rem(r, nb)}

    barrier = pltpu.get_barrier_semaphore()
    pl.semaphore_signal(barrier, inc=1, device_id={"weights": 1 - p},
                        device_id_type=pl.DeviceIdType.MESH)

    @pl.loop(1, n)
    def _(d):
        pl.semaphore_signal(barrier, inc=1, device_id=place(d)[1],
                            device_id_type=pl.DeviceIdType.MESH)

    pl.semaphore_wait(barrier, n)

    swap = pltpu.make_async_remote_copy(
        src_ref=parts.at[1 - p], dst_ref=near, send_sem=sem.at[0], recv_sem=sem.at[1],
        device_id={"weights": 1 - p}, device_id_type=pl.DeviceIdType.MESH)
    swap.start()
    swap.wait()
    total[...] = parts[p] + near[...]

    def scatter(d):
        r, to = place(d)
        return pltpu.make_async_remote_copy(
            src_ref=total.at[pl.ds(pl.multiple_of(r * chunk, 8), chunk)],
            dst_ref=slots.at[d - 1], send_sem=send.at[d - 1], recv_sem=recv.at[d - 1],
            device_id=to, device_id_type=pl.DeviceIdType.MESH)

    @pl.loop(1, n)
    def _(d):
        scatter(d).start()

    own = pl.ds(pl.multiple_of(me * chunk, 8), chunk)
    full[own] = total[own]

    @pl.loop(1, n)
    def _(d):
        scatter(d).wait_recv()
        full[own] += slots[d - 1]

    def gather(d, row):
        return pltpu.make_async_remote_copy(
            src_ref=full.at[own],
            dst_ref=full.at[pl.ds(pl.multiple_of(row * chunk, 8), chunk)],
            send_sem=send2.at[d - 1], recv_sem=recv2.at[d - 1],
            device_id=place(d)[1], device_id_type=pl.DeviceIdType.MESH)

    @pl.loop(1, n)
    def _(d):
        gather(d, me).start()

    @pl.loop(1, n)
    def _(d):
        gather(d, lax.rem(me + n - d, n)).wait_recv()

    @pl.loop(1, n)
    def _(d):
        scatter(d).wait_send()
        gather(d, me).wait_send()


def total_panel(parts):
    rows, C = parts.shape[1:]
    n = lax.axis_size("batch") * lax.axis_size("tm")
    f32 = jnp.float32
    dma = pltpu.SemaphoreType.DMA
    return pl.pallas_call(
        reduce_kernel,
        out_shape=jax.ShapeDtypeStruct((rows, C), f32),
        in_specs=[pl.BlockSpec(memory_space=pltpu.VMEM)],
        out_specs=pl.BlockSpec(memory_space=pltpu.VMEM),
        scratch_shapes=[
            pltpu.VMEM((rows, C), f32),
            pltpu.VMEM((rows, C), f32),
            pltpu.VMEM((n - 1, rows // n, C), f32),
            dma((2,)), dma((n - 1,)), dma((n - 1,)), dma((n - 1,)), dma((n - 1,)),
        ],
        compiler_params=pltpu.CompilerParams(
            collective_id=1, has_side_effects=True, vmem_limit_bytes=24 * 2**20),
    )(parts)


def shards(x, te, starts, lengths, wc, bc, wm, bm, wd, bd):
    B, T, C = x.shape
    N, CO = te.shape[1:]
    xl, xr, tl, tr = halos(x, te)
    mine = lax.axis_index(("weights", "batch")) * B
    own = jnp.stack([lax.dynamic_slice_in_dim(starts, mine, B),
                     lax.dynamic_slice_in_dim(lengths, mine, B)], axis=1).reshape(-1)
    tm = lax.axis_index("tm").astype(jnp.int32)
    head = jnp.stack([jnp.int32(0), jnp.int32(0), jnp.int32(lax.axis_size("tm")), tm])
    bounds = jnp.concatenate([head, own]).astype(jnp.int32)
    n = lax.axis_size("batch") * lax.axis_size("tm")
    rows = -(-(8 * C + 8) // (8 * n)) * 8 * n
    parts = local_grads(
        rows, bounds, x, xl, xr, te, tl, tr, wc, bc.reshape(1, C), wm, bm.reshape(1, C),
        wd, bd.reshape(1, CO))
    scale = 1.0 / (jnp.sum(lengths).astype(jnp.float32) * CO)
    g = total_panel(parts)
    s = g * (2.0 * scale)
    h = C // 2
    low = s[:4 * C, :h].reshape(4, C, h)
    high = s[:3 * C, h:].reshape(3, C, h)
    g_conv = jnp.stack([low[0], high[0], low[1], high[1], low[2], high[2], low[3]])
    g_mix = jnp.concatenate([s[3 * C:3 * C + h, h:], s[3 * C + h:4 * C, h:]], axis=1)
    return (
        g_conv,
        s[8 * C + 1, h:],
        g_mix,
        s[8 * C + 1, :h],
        s[4 * C:8 * C].reshape(4, C, C),
        s[8 * C],
        (jnp.sum(g[8 * C + 2]) * scale).reshape(1),
    )


def solution(mesh):
    clips = P(("groups", "weights", "batch"), "tm", None)
    return jax.shard_map(
        shards,
        mesh=mesh,
        in_specs=(clips, clips, P("groups"), P("groups")) + (P(),) * 6,
        out_specs=(
            P("groups", None, "weights"),
            P(("groups", "weights")),
            P(("groups", "weights"), None),
            P(("groups", "weights")),
            P("groups", None, "weights"),
            P(("groups", "weights")),
            P("groups"),
        ),
        check_vma=False,
    )
```

```python
import functools

import jax
import jax.numpy as jnp
from jax import lax
from jax.experimental import pallas as pl
from jax.experimental.pallas import tpu as pltpu
from jax.sharding import PartitionSpec as P

TAPS = 7
RATE = 9
HALO = 32
LEAD = 40
EDGE = 24
CHUNK = 256


def elu(v):
    return jnp.where(v > 0, v, jnp.exp(jnp.minimum(v, 0.0)) - 1.0)


def slope(e):
    return jnp.where(e > 0, 1.0, e + 1.0)


def split(a):
    hi = a.astype(jnp.bfloat16)
    return hi, (a - hi.astype(jnp.float32)).astype(jnp.bfloat16)


def three(a, b, dims):
    def dot(u, v):
        return lax.dot_general(u, v, (dims, ((), ())), preferred_element_type=jnp.float32)

    return dot(a[0], b[0]) + dot(a[1], b[0]) + dot(a[0], b[1])


def mm(a, w):
    return three(split(a), (w[0], w[1]), ((1,), (0,)))


def mm_t(a, b):
    return three(split(a), split(b), ((0,), (0,)))


def local_kernel(
    starts, lengths, x, xl, xr, te, tl, tr, wc, bc, wm, bm, wd, bd,
    o_all,
    o_mix, o_bias, act, ya, yb, hid, sec, d0, d1, dsec, dhid, w2, wb, wf, wx, acc2, accd,
):
    step = pl.program_id(0)
    steps = pl.num_programs(0)
    T, C = x.shape[1], x.shape[2]
    N, CO = te.shape[1], te.shape[2]
    tm = lax.axis_index("tm")
    t0, j0 = tm * T, tm * N
    total = lax.axis_size("tm") * T
    clip = lax.axis_index(("weights", "batch")) * steps + step
    first = starts[clip]
    last = first + lengths[clip]

    @pl.when(step == 0)
    def _():
        def put(w, rows, cols, value):
            hi, lo = split(value)
            w[0, rows, cols] = hi
            w[1, rows, cols] = lo

        for k in range(TAPS + 1):
            m, p = k // 2, k % 2
            put(w2, slice(m * C, (m + 1) * C), slice(p * C, (p + 1) * C),
                wc[k] if k < TAPS else jnp.zeros((C, C), jnp.float32))
        for k in range(4):
            r, p = k // 2, k % 2
            put(wb, slice(r * CO, (r + 1) * CO), slice(p * C, (p + 1) * C), wd[k].T)
            put(wf, slice(k * C, (k + 1) * C), slice(0, CO), wd[k])
        put(wx, slice(0, C), slice(0, C), wm[...])
        put(wx, slice(C, 2 * C), slice(0, C), wm[...].T)
        acc2[...] = jnp.zeros_like(acc2)
        accd[...] = jnp.zeros_like(accd)
        o_mix[...] = jnp.zeros_like(o_mix)
        o_bias[...] = jnp.zeros_like(o_bias)
        dhid[...] = jnp.zeros_like(dhid)
        act[0:8] = jnp.zeros((8, C), jnp.float32)
        act[LEAD + T + HALO:] = jnp.zeros_like(act[LEAD + T + HALO:])
        sec[0:EDGE] = jnp.zeros((EDGE, C), jnp.float32)
        sec[EDGE + T + 8:] = jnp.zeros_like(sec[EDGE + T + 8:])

    act[8:LEAD] = elu(xl[0])
    act[LEAD + T:LEAD + T + HALO] = elu(xr[0])

    @pl.loop(0, T // CHUNK)
    def _(i):
        s = pl.multiple_of(i * CHUNK, CHUNK)
        act[pl.ds(LEAD + s, CHUNK)] = elu(x[0, pl.ds(s, CHUNK)])

    def conv(t, n):
        a = jnp.concatenate(
            [act[pl.ds(LEAD - 27 + 18 * m + t, n)] for m in range(4)], axis=1)
        r = mm(a, w2)
        row = pl.ds(8 + t, n)
        ya[row] = r[:, :C]
        yb[row] = r[:, C:]

    @pl.loop(0, T // CHUNK)
    def _(i):
        conv(i * CHUNK - 8, CHUNK)

    conv(T - 8, 32)

    def section(t, n, xv):
        h = ya[pl.ds(8 + t, n)] + yb[pl.ds(17 + t, n)] + bc[...]
        g = elu(h)
        hid[pl.ds(8 + t, n)] = g
        v = elu(xv + mm(g, (wx[0, :C], wx[1, :C])) + bm[...])
        pos = t0 + t + lax.broadcasted_iota(jnp.int32, (n, C), 0)
        sec[pl.ds(EDGE + t, n)] = jnp.where((pos >= 0) & (pos < total), v, 0.0)

    section(-8, 8, xl[0, HALO - 8:])
    section(T, 8, xr[0, :8])

    @pl.loop(0, T // CHUNK)
    def _(i):
        s = pl.multiple_of(i * CHUNK, CHUNK)
        section(s, CHUNK, x[0, pl.ds(s, CHUNK)])

    def error(j, n, tv):
        a = jnp.concatenate(
            [sec[pl.ds(EDGE + 2 * j + k - 1, n, stride=2)] for k in range(4)], axis=1)
        e = mm(a, wf) + bd[...] - tv
        pos = j0 + j + lax.broadcasted_iota(jnp.int32, (n, CO), 0)
        d = jnp.where((pos >= first) & (pos < last), e, 0.0)
        d0[pl.ds(8 + j, n)] = d[:, :C]
        d1[pl.ds(8 + j, n)] = d[:, C:]
        return a, d

    error(-8, 8, tl[0])
    error(N, 8, tr[0])

    @pl.loop(0, N // CHUNK)
    def _(i):
        s = pl.multiple_of(i * CHUNK, CHUNK)
        a, d = error(s, CHUNK, te[0, pl.ds(s, CHUNK)])
        accd[...] += mm_t(a, d)
        o_bias[0:1, :] += jnp.sum(d, axis=0, keepdims=True)
        o_bias[1:2, :] += jnp.sum(d * d, axis=0, keepdims=True)

    def back(j, n):
        b = jnp.concatenate(
            [d0[pl.ds(8 + j, n)], d1[pl.ds(8 + j, n)],
             d0[pl.ds(7 + j, n)], d1[pl.ds(7 + j, n)]], axis=1)
        r = mm(b, wb)
        dsec[pl.ds(EDGE + 2 * j - 1, n, stride=2)] = r[:, :C]
        dsec[pl.ds(EDGE + 2 * j, n, stride=2)] = r[:, C:]

    @pl.loop(0, N // CHUNK)
    def _(i):
        back(pl.multiple_of(i * CHUNK, CHUNK), CHUNK)

    back(N, 8)

    @pl.loop(0, T // CHUNK)
    def _(i):
        s = pl.multiple_of(i * CHUNK, CHUNK)
        ds = dsec[pl.ds(EDGE + s, CHUNK)] * slope(sec[pl.ds(EDGE + s, CHUNK)])
        g = hid[pl.ds(8 + s, CHUNK)]
        o_mix[...] += mm_t(g, ds)
        dg = mm(ds, (wx[0, C:], wx[1, C:]))
        dh = dg * slope(g)
        dhid[pl.ds(16 + s, CHUNK)] = dh
        o_bias[2:3, :C] += jnp.sum(ds, axis=0, keepdims=True)
        o_bias[2:3, C:] += jnp.sum(dh, axis=0, keepdims=True)

    def taps(t, n):
        a = jnp.concatenate(
            [act[pl.ds(LEAD - 27 + 18 * m + t, n)] for m in range(4)], axis=1)
        d = jnp.concatenate(
            [dhid[pl.ds(16 + t, n)], dhid[pl.ds(7 + t, n)]], axis=1)
        acc2[...] += mm_t(a, d)

    @pl.loop(0, T // CHUNK)
    def _(i):
        taps(pl.multiple_of(i * CHUNK, CHUNK), CHUNK)

    taps(T, 16)

    @pl.when(step == steps - 1)
    def _():
        h = C // 2
        count = lax.fori_loop(
            0, lengths.shape[0], lambda i, c: c + lengths[i], jnp.int32(0))
        scale = 1.0 / (jnp.full((1, C), count.astype(jnp.float32)) * CO)
        two = 2.0 * scale
        for p in range(2):
            c = slice(p * h, (p + 1) * h)
            d = slice(C + p * h, C + (p + 1) * h)
            o_all[p, 0:4 * C, :h] = acc2[:, c] * two[:, :h]
            o_all[p, 0:3 * C, h:] = acc2[0:3 * C, d] * two[:, :h]
            o_all[p, 3 * C:3 * C + h, h:] = o_mix[c, :h] * two[:, :h]
            o_all[p, 3 * C + h:4 * C, h:] = o_mix[c, h:] * two[:, :h]
            o_all[p, 4 * C:8 * C] = accd[:, p * C:(p + 1) * C] * two
            o_all[p, 8 * C:] = jnp.zeros_like(o_all[p, 8 * C:])
            o_all[p, 8 * C:8 * C + 1] = o_bias[0:1, p * C:(p + 1) * C] * two
            o_all[p, 8 * C + 1:8 * C + 2, :h] = o_bias[2:3, c] * two[:, :h]
            o_all[p, 8 * C + 2:8 * C + 3, :h] = o_bias[2:3, d] * two[:, :h]
            o_all[p, 8 * C + 3:8 * C + 4] = (o_bias[1:2, :C] + o_bias[1:2, C:]) * scale


def local_grads(rows, starts, lengths, x, xl, xr, te, tl, tr, wc, bc, wm, bm, wd, bd):
    B, T, C = x.shape
    N, CO = te.shape[1:]
    f32 = jnp.float32

    def clip(a):
        return pl.BlockSpec((1,) + a.shape[1:], lambda i, *_: (i, 0, 0))

    def whole(a):
        return pl.BlockSpec(a.shape, lambda i, *_: (0,) * len(a.shape))

    out = jax.ShapeDtypeStruct((2, rows, C), f32)
    return pl.pallas_call(
        local_kernel,
        out_shape=out,
        grid_spec=pltpu.PrefetchScalarGridSpec(
            num_scalar_prefetch=2,
            grid=(B,),
            in_specs=[clip(a) for a in (x, xl, xr, te, tl, tr)]
            + [whole(a) for a in (wc, bc, wm, bm, wd, bd)],
            out_specs=whole(out),
            scratch_shapes=[
                pltpu.VMEM((C, C), f32),
                pltpu.VMEM((8, CO), f32),
                pltpu.VMEM((LEAD + T + HALO + 56, C), f32),
                pltpu.VMEM((T + 32, C), f32),
                pltpu.VMEM((T + 32, C), f32),
                pltpu.VMEM((T + 16, C), f32),
                pltpu.VMEM((EDGE + T + 32, C), f32),
                pltpu.VMEM((N + 16, CO // 2), f32),
                pltpu.VMEM((N + 16, CO // 2), f32),
                pltpu.VMEM((EDGE + T + 32, C), f32),
                pltpu.VMEM((T + 32, C), f32),
                pltpu.VMEM((2, 4 * C, 2 * C), jnp.bfloat16),
                pltpu.VMEM((2, 2 * CO, 2 * C), jnp.bfloat16),
                pltpu.VMEM((2, 4 * C, CO), jnp.bfloat16),
                pltpu.VMEM((2, 2 * C, C), jnp.bfloat16),
                pltpu.VMEM((4 * C, 2 * C), f32),
                pltpu.VMEM((4 * C, CO), f32),
            ],
        ),
        compiler_params=pltpu.CompilerParams(vmem_limit_bytes=58 * 2**20),
    )(starts, lengths, x, xl, xr, te, tl, tr, wc, bc, wm, bm, wd, bd)


def halo_kernel(x, te, xl, xr, tl, tr, sxl, sxr, stl, str_, send, recv):
    count = lax.axis_size("tm")
    tm = lax.axis_index("tm")
    T, N = x.shape[1], te.shape[1]
    has_left, has_right = tm > 0, tm < count - 1
    barrier = pltpu.get_barrier_semaphore()

    def copy(k, src, dst, to):
        return pltpu.make_async_remote_copy(
            src_ref=src, dst_ref=dst, send_sem=send.at[k], recv_sem=recv.at[k],
            device_id={"tm": to}, device_id_type=pl.DeviceIdType.MESH)

    up = [copy(0, x.at[:, pl.ds(T - HALO, HALO)], sxl, tm + 1),
          copy(1, te.at[:, pl.ds(N - 8, 8)], stl, tm + 1)]
    down = [copy(2, x.at[:, pl.ds(0, HALO)], sxr, tm - 1),
            copy(3, te.at[:, pl.ds(0, 8)], str_, tm - 1)]

    @pl.when(has_left)
    def _():
        pl.semaphore_signal(barrier, inc=1, device_id={"tm": tm - 1},
                            device_id_type=pl.DeviceIdType.MESH)

    @pl.when(has_right)
    def _():
        pl.semaphore_signal(barrier, inc=1, device_id={"tm": tm + 1},
                            device_id_type=pl.DeviceIdType.MESH)

    pl.semaphore_wait(barrier, has_left.astype(jnp.int32) + has_right.astype(jnp.int32))

    @pl.when(has_right)
    def _():
        for c in up:
            c.start()

    @pl.when(has_left)
    def _():
        for c in down:
            c.start()

    @pl.when(has_left)
    def _():
        for c in up:
            c.wait_recv()
        xl[...] = sxl[...]
        tl[...] = stl[...]

    @pl.when(tm == 0)
    def _():
        xl[...] = jnp.zeros_like(xl)
        tl[...] = jnp.zeros_like(tl)

    @pl.when(has_right)
    def _():
        for c in down:
            c.wait_recv()
        xr[...] = sxr[...]
        tr[...] = str_[...]

    @pl.when(tm == count - 1)
    def _():
        xr[...] = jnp.zeros_like(xr)
        tr[...] = jnp.zeros_like(tr)

    @pl.when(has_right)
    def _():
        for c in up:
            c.wait_send()

    @pl.when(has_left)
    def _():
        for c in down:
            c.wait_send()


def halos(x, te):
    B, T, C = x.shape
    CO = te.shape[2]
    shapes = [(B, HALO, C), (B, HALO, C), (B, 8, CO), (B, 8, CO)]
    return pl.pallas_call(
        halo_kernel,
        out_shape=[jax.ShapeDtypeStruct(s, jnp.float32) for s in shapes],
        in_specs=[pl.BlockSpec(memory_space=pl.ANY)] * 2,
        out_specs=[pl.BlockSpec(memory_space=pltpu.VMEM)] * 4,
        scratch_shapes=[pltpu.VMEM(s, jnp.float32) for s in shapes]
        + [pltpu.SemaphoreType.DMA((4,)), pltpu.SemaphoreType.DMA((4,))],
        compiler_params=pltpu.CompilerParams(
            collective_id=0, has_side_effects=True, vmem_limit_bytes=58 * 2**20),
    )(x, te)


def reduce_kernel(parts, full, near, total, slots, ssend, srecv, send, recv, send2, recv2):
    p = lax.axis_index("weights")
    nb, n = lax.axis_size("batch"), lax.axis_size("batch") * lax.axis_size("tm")
    me = lax.axis_index("tm") * nb + lax.axis_index("batch")
    chunk = full.shape[0] // n

    def place(d):
        r = lax.rem(me + d, n)
        return r, {"tm": r // nb, "batch": lax.rem(r, nb)}

    barrier = pltpu.get_barrier_semaphore()
    pl.semaphore_signal(barrier, inc=1, device_id={"weights": 1 - p},
                        device_id_type=pl.DeviceIdType.MESH)

    @pl.loop(1, n)
    def _(d):
        pl.semaphore_signal(barrier, inc=1, device_id=place(d)[1],
                            device_id_type=pl.DeviceIdType.MESH)

    pl.semaphore_wait(barrier, n)

    def rows(d):
        r = lax.rem(me + d, n)
        return pl.ds(pl.multiple_of(r * chunk, 8), chunk)

    def swap(d):
        return pltpu.make_async_remote_copy(
            src_ref=parts.at[1 - p, rows(d)], dst_ref=near.at[rows(d)],
            send_sem=ssend.at[d - 1], recv_sem=srecv.at[d - 1],
            device_id={"weights": 1 - p}, device_id_type=pl.DeviceIdType.MESH)

    @pl.loop(1, n + 1)
    def _(d):
        swap(d).start()

    def scatter(d):
        r, to = place(d)
        return pltpu.make_async_remote_copy(
            src_ref=total.at[pl.ds(pl.multiple_of(r * chunk, 8), chunk)],
            dst_ref=slots.at[d - 1], send_sem=send.at[d - 1], recv_sem=recv.at[d - 1],
            device_id=to, device_id_type=pl.DeviceIdType.MESH)

    @pl.loop(1, n)
    def _(d):
        swap(d).wait_recv()
        total[rows(d)] = parts[p, rows(d)] + near[rows(d)]
        scatter(d).start()

    own = pl.ds(pl.multiple_of(me * chunk, 8), chunk)
    swap(n).wait_recv()
    full[own] = parts[p, own] + near[own]

    @pl.loop(1, n)
    def _(d):
        scatter(d).wait_recv()
        full[own] += slots[d - 1]

    def gather(d, row):
        return pltpu.make_async_remote_copy(
            src_ref=full.at[own],
            dst_ref=full.at[pl.ds(pl.multiple_of(row * chunk, 8), chunk)],
            send_sem=send2.at[d - 1], recv_sem=recv2.at[d - 1],
            device_id=place(d)[1], device_id_type=pl.DeviceIdType.MESH)

    @pl.loop(1, n)
    def _(d):
        gather(d, me).start()

    @pl.loop(1, n)
    def _(d):
        gather(d, lax.rem(me + n - d, n)).wait_recv()

    @pl.loop(1, n)
    def _(d):
        scatter(d).wait_send()
        gather(d, me).wait_send()

    @pl.loop(1, n + 1)
    def _(d):
        swap(d).wait_send()


def total_panel(parts):
    rows, C = parts.shape[1:]
    n = lax.axis_size("batch") * lax.axis_size("tm")
    f32 = jnp.float32
    dma = pltpu.SemaphoreType.DMA
    return pl.pallas_call(
        reduce_kernel,
        out_shape=jax.ShapeDtypeStruct((rows, C), f32),
        in_specs=[pl.BlockSpec(memory_space=pltpu.VMEM)],
        out_specs=pl.BlockSpec(memory_space=pltpu.VMEM),
        scratch_shapes=[
            pltpu.VMEM((rows, C), f32),
            pltpu.VMEM((rows, C), f32),
            pltpu.VMEM((n - 1, rows // n, C), f32),
            dma((n,)), dma((n,)), dma((n - 1,)), dma((n - 1,)), dma((n - 1,)), dma((n - 1,)),
        ],
        compiler_params=pltpu.CompilerParams(
            collective_id=1, has_side_effects=True, vmem_limit_bytes=24 * 2**20),
    )(parts)


def unpack_kernel(g, conv, conv_b, mix, mix_b, down, down_b, loss):
    C = g.shape[1]
    h = C // 2
    for k in range(TAPS):
        m = k // 2
        conv[k] = g[m * C:(m + 1) * C, (k % 2) * h:(k % 2 + 1) * h]
    mix[:, :h] = g[3 * C:3 * C + h, h:]
    mix[:, h:] = g[3 * C + h:4 * C, h:]
    for k in range(4):
        down[k] = g[(4 + k) * C:(5 + k) * C]
    down_b[...] = g[8 * C:8 * C + 1]
    mix_b[...] = g[8 * C + 1:8 * C + 2, :h]
    conv_b[...] = g[8 * C + 2:8 * C + 3, :h]
    loss[...] = jnp.sum(g[8 * C + 3:8 * C + 4], axis=1, keepdims=True)


def unpack(g):
    C = g.shape[1]
    h = C // 2
    shapes = [(TAPS, C, h), (1, h), (h, C), (1, h), (4, C, C), (1, C), (1, 1)]
    vmem = pl.BlockSpec(memory_space=pltpu.VMEM)
    return pl.pallas_call(
        unpack_kernel,
        out_shape=[jax.ShapeDtypeStruct(s, jnp.float32) for s in shapes],
        in_specs=[vmem],
        out_specs=[vmem] * len(shapes),
        compiler_params=pltpu.CompilerParams(vmem_limit_bytes=16 * 2**20),
    )(g)


def shards(x, te, starts, lengths, wc, bc, wm, bm, wd, bd):
    C, CO = x.shape[2], te.shape[2]
    xl, xr, tl, tr = halos(x, te)
    n = lax.axis_size("batch") * lax.axis_size("tm")
    rows = -(-(8 * C + 8) // (8 * n)) * 8 * n
    parts = local_grads(
        rows, starts, lengths, x, xl, xr, te, tl, tr, wc, bc.reshape(1, C), wm,
        bm.reshape(1, C), wd, bd.reshape(1, CO))
    conv, conv_b, mix, mix_b, down, down_b, loss = unpack(total_panel(parts))
    return (conv, conv_b.reshape(-1), mix, mix_b.reshape(-1), down,
            down_b.reshape(-1), loss.reshape(1))


def solution(mesh):
    clips = P(("groups", "weights", "batch"), "tm", None)
    return jax.shard_map(
        shards,
        mesh=mesh,
        in_specs=(clips, clips, P("groups"), P("groups")) + (P(),) * 6,
        out_specs=(
            P("groups", None, "weights"),
            P(("groups", "weights")),
            P(("groups", "weights"), None),
            P(("groups", "weights")),
            P("groups", None, "weights"),
            P(("groups", "weights")),
            P("groups"),
        ),
        check_vma=False,
    )
```

```python
import functools

import jax
import jax.numpy as jnp
from jax import lax
from jax.experimental import pallas as pl
from jax.experimental.pallas import tpu as pltpu
from jax.sharding import PartitionSpec as P

TAPS = 7
RATE = 9
HALO = 32
LEAD = 40
EDGE = 24
CHUNK = 1024


def elu(v):
    return jnp.where(v > 0, v, jnp.exp(jnp.minimum(v, 0.0)) - 1.0)


def slope(e):
    return jnp.where(e > 0, 1.0, e + 1.0)


def split(a):
    hi = a.astype(jnp.bfloat16)
    return hi, (a - hi.astype(jnp.float32)).astype(jnp.bfloat16)


def three(a, b, dims):
    def dot(u, v):
        return lax.dot_general(u, v, (dims, ((), ())), preferred_element_type=jnp.float32)

    return dot(a[0], b[0]) + dot(a[1], b[0]) + dot(a[0], b[1])


def mm(a, w):
    return three(split(a), (w[0], w[1]), ((1,), (0,)))


def mm_t(a, b):
    return three(split(a), split(b), ((0,), (0,)))


def local_kernel(
    starts, lengths, x, xl, xr, te, tl, tr, wc, bc, wm, bm, wd, bd,
    o_all,
    o_mix, o_bias, act, ya, yb, hid, sec, d0, d1, dsec, dhid, w2, wb, wf, wx, acc2, accd,
):
    step = pl.program_id(0)
    steps = pl.num_programs(0)
    T, C = x.shape[1], x.shape[2]
    N, CO = te.shape[1], te.shape[2]
    tm = lax.axis_index("tm")
    t0, j0 = tm * T, tm * N
    total = lax.axis_size("tm") * T
    clip = lax.axis_index(("weights", "batch")) * steps + step
    first = starts[clip]
    last = first + lengths[clip]

    @pl.when(step == 0)
    def _():
        def put(w, rows, cols, value):
            hi, lo = split(value)
            w[0, rows, cols] = hi
            w[1, rows, cols] = lo

        for k in range(TAPS + 1):
            m, p = k // 2, k % 2
            put(w2, slice(m * C, (m + 1) * C), slice(p * C, (p + 1) * C),
                wc[k] if k < TAPS else jnp.zeros((C, C), jnp.float32))
        for k in range(4):
            r, p = k // 2, k % 2
            put(wb, slice(r * CO, (r + 1) * CO), slice(p * C, (p + 1) * C), wd[k].T)
            put(wf, slice(k * C, (k + 1) * C), slice(0, CO), wd[k])
        put(wx, slice(0, C), slice(0, C), wm[...])
        put(wx, slice(C, 2 * C), slice(0, C), wm[...].T)
        acc2[...] = jnp.zeros_like(acc2)
        accd[...] = jnp.zeros_like(accd)
        o_mix[...] = jnp.zeros_like(o_mix)
        o_bias[...] = jnp.zeros_like(o_bias)
        dhid[...] = jnp.zeros_like(dhid)
        act[0:8] = jnp.zeros((8, C), jnp.float32)
        act[LEAD + T + HALO:] = jnp.zeros_like(act[LEAD + T + HALO:])
        sec[0:EDGE] = jnp.zeros((EDGE, C), jnp.float32)
        sec[EDGE + T + 8:] = jnp.zeros_like(sec[EDGE + T + 8:])

    act[8:LEAD] = elu(xl[0])
    act[LEAD + T:LEAD + T + HALO] = elu(xr[0])

    @pl.loop(0, T // CHUNK)
    def _(i):
        s = pl.multiple_of(i * CHUNK, CHUNK)
        act[pl.ds(LEAD + s, CHUNK)] = elu(x[0, pl.ds(s, CHUNK)])

    def conv(t, n):
        a = jnp.concatenate(
            [act[pl.ds(LEAD - 27 + 18 * m + t, n)] for m in range(4)], axis=1)
        r = mm(a, w2)
        row = pl.ds(8 + t, n)
        ya[row] = r[:, :C]
        yb[row] = r[:, C:]

    @pl.loop(0, T // CHUNK)
    def _(i):
        conv(i * CHUNK - 8, CHUNK)

    conv(T - 8, 32)

    def section(t, n, xv):
        h = ya[pl.ds(8 + t, n)] + yb[pl.ds(17 + t, n)] + bc[...]
        g = elu(h)
        hid[pl.ds(8 + t, n)] = g
        v = elu(xv + mm(g, (wx[0, :C], wx[1, :C])) + bm[...])
        pos = t0 + t + lax.broadcasted_iota(jnp.int32, (n, C), 0)
        sec[pl.ds(EDGE + t, n)] = jnp.where((pos >= 0) & (pos < total), v, 0.0)

    section(-8, 8, xl[0, HALO - 8:])
    section(T, 8, xr[0, :8])

    @pl.loop(0, T // CHUNK)
    def _(i):
        s = pl.multiple_of(i * CHUNK, CHUNK)
        section(s, CHUNK, x[0, pl.ds(s, CHUNK)])

    def error(j, n, tv):
        a = jnp.concatenate(
            [sec[pl.ds(EDGE + 2 * j + k - 1, n, stride=2)] for k in range(4)], axis=1)
        e = mm(a, wf) + bd[...] - tv
        pos = j0 + j + lax.broadcasted_iota(jnp.int32, (n, CO), 0)
        d = jnp.where((pos >= first) & (pos < last), e, 0.0)
        d0[pl.ds(8 + j, n)] = d[:, :C]
        d1[pl.ds(8 + j, n)] = d[:, C:]
        return a, d

    error(-8, 8, tl[0])
    error(N, 8, tr[0])

    @pl.loop(0, N // CHUNK)
    def _(i):
        s = pl.multiple_of(i * CHUNK, CHUNK)
        a, d = error(s, CHUNK, te[0, pl.ds(s, CHUNK)])
        accd[...] += mm_t(a, d)
        o_bias[0:1, :] += jnp.sum(d, axis=0, keepdims=True)
        o_bias[1:2, :] += jnp.sum(d * d, axis=0, keepdims=True)

    def back(j, n):
        b = jnp.concatenate(
            [d0[pl.ds(8 + j, n)], d1[pl.ds(8 + j, n)],
             d0[pl.ds(7 + j, n)], d1[pl.ds(7 + j, n)]], axis=1)
        r = mm(b, wb)
        dsec[pl.ds(EDGE + 2 * j - 1, n, stride=2)] = r[:, :C]
        dsec[pl.ds(EDGE + 2 * j, n, stride=2)] = r[:, C:]

    @pl.loop(0, N // CHUNK)
    def _(i):
        back(pl.multiple_of(i * CHUNK, CHUNK), CHUNK)

    back(N, 8)

    @pl.loop(0, T // CHUNK)
    def _(i):
        s = pl.multiple_of(i * CHUNK, CHUNK)
        ds = dsec[pl.ds(EDGE + s, CHUNK)] * slope(sec[pl.ds(EDGE + s, CHUNK)])
        g = hid[pl.ds(8 + s, CHUNK)]
        o_mix[...] += mm_t(g, ds)
        dg = mm(ds, (wx[0, C:], wx[1, C:]))
        dh = dg * slope(g)
        dhid[pl.ds(16 + s, CHUNK)] = dh
        o_bias[2:3, :C] += jnp.sum(ds, axis=0, keepdims=True)
        o_bias[2:3, C:] += jnp.sum(dh, axis=0, keepdims=True)

    def taps(t, n):
        a = jnp.concatenate(
            [act[pl.ds(LEAD - 27 + 18 * m + t, n)] for m in range(4)], axis=1)
        d = jnp.concatenate(
            [dhid[pl.ds(16 + t, n)], dhid[pl.ds(7 + t, n)]], axis=1)
        acc2[...] += mm_t(a, d)

    @pl.loop(0, T // CHUNK)
    def _(i):
        taps(pl.multiple_of(i * CHUNK, CHUNK), CHUNK)

    taps(T, 16)

    @pl.when(step == steps - 1)
    def _():
        h = C // 2
        count = lax.fori_loop(
            0, lengths.shape[0], lambda i, c: c + lengths[i], jnp.int32(0))
        scale = 1.0 / (jnp.full((1, C), count.astype(jnp.float32)) * CO)
        two = 2.0 * scale
        for p in range(2):
            c = slice(p * h, (p + 1) * h)
            d = slice(C + p * h, C + (p + 1) * h)
            o_all[p, 0:4 * C, :h] = acc2[:, c] * two[:, :h]
            o_all[p, 0:3 * C, h:] = acc2[0:3 * C, d] * two[:, :h]
            o_all[p, 3 * C:3 * C + h, h:] = o_mix[c, :h] * two[:, :h]
            o_all[p, 3 * C + h:4 * C, h:] = o_mix[c, h:] * two[:, :h]
            o_all[p, 4 * C:8 * C] = accd[:, p * C:(p + 1) * C] * two
            o_all[p, 8 * C:] = jnp.zeros_like(o_all[p, 8 * C:])
            o_all[p, 8 * C:8 * C + 1] = o_bias[0:1, p * C:(p + 1) * C] * two
            o_all[p, 8 * C + 1:8 * C + 2, :h] = o_bias[2:3, c] * two[:, :h]
            o_all[p, 8 * C + 2:8 * C + 3, :h] = o_bias[2:3, d] * two[:, :h]
            o_all[p, 8 * C + 3:8 * C + 4] = (o_bias[1:2, :C] + o_bias[1:2, C:]) * scale


def local_grads(rows, starts, lengths, x, xl, xr, te, tl, tr, wc, bc, wm, bm, wd, bd):
    B, T, C = x.shape
    N, CO = te.shape[1:]
    f32 = jnp.float32

    def clip(a):
        return pl.BlockSpec((1,) + a.shape[1:], lambda i, *_: (i, 0, 0))

    def whole(a):
        return pl.BlockSpec(a.shape, lambda i, *_: (0,) * len(a.shape))

    out = jax.ShapeDtypeStruct((2, rows, C), f32)
    return pl.pallas_call(
        local_kernel,
        out_shape=out,
        grid_spec=pltpu.PrefetchScalarGridSpec(
            num_scalar_prefetch=2,
            grid=(B,),
            in_specs=[clip(a) for a in (x, xl, xr, te, tl, tr)]
            + [whole(a) for a in (wc, bc, wm, bm, wd, bd)],
            out_specs=whole(out),
            scratch_shapes=[
                pltpu.VMEM((C, C), f32),
                pltpu.VMEM((8, CO), f32),
                pltpu.VMEM((LEAD + T + HALO + 56, C), f32),
                pltpu.VMEM((T + 32, C), f32),
                pltpu.VMEM((T + 32, C), f32),
                pltpu.VMEM((T + 16, C), f32),
                pltpu.VMEM((EDGE + T + 32, C), f32),
                pltpu.VMEM((N + 16, CO // 2), f32),
                pltpu.VMEM((N + 16, CO // 2), f32),
                pltpu.VMEM((EDGE + T + 32, C), f32),
                pltpu.VMEM((T + 32, C), f32),
                pltpu.VMEM((2, 4 * C, 2 * C), jnp.bfloat16),
                pltpu.VMEM((2, 2 * CO, 2 * C), jnp.bfloat16),
                pltpu.VMEM((2, 4 * C, CO), jnp.bfloat16),
                pltpu.VMEM((2, 2 * C, C), jnp.bfloat16),
                pltpu.VMEM((4 * C, 2 * C), f32),
                pltpu.VMEM((4 * C, CO), f32),
            ],
        ),
        compiler_params=pltpu.CompilerParams(vmem_limit_bytes=58 * 2**20),
    )(starts, lengths, x, xl, xr, te, tl, tr, wc, bc, wm, bm, wd, bd)


def halo_kernel(x, te, xl, xr, tl, tr, sxl, sxr, stl, str_, send, recv):
    count = lax.axis_size("tm")
    tm = lax.axis_index("tm")
    T, N = x.shape[1], te.shape[1]
    has_left, has_right = tm > 0, tm < count - 1
    barrier = pltpu.get_barrier_semaphore()

    def copy(k, src, dst, to):
        return pltpu.make_async_remote_copy(
            src_ref=src, dst_ref=dst, send_sem=send.at[k], recv_sem=recv.at[k],
            device_id={"tm": to}, device_id_type=pl.DeviceIdType.MESH)

    up = [copy(0, x.at[:, pl.ds(T - HALO, HALO)], sxl, tm + 1),
          copy(1, te.at[:, pl.ds(N - 8, 8)], stl, tm + 1)]
    down = [copy(2, x.at[:, pl.ds(0, HALO)], sxr, tm - 1),
            copy(3, te.at[:, pl.ds(0, 8)], str_, tm - 1)]

    @pl.when(has_left)
    def _():
        pl.semaphore_signal(barrier, inc=1, device_id={"tm": tm - 1},
                            device_id_type=pl.DeviceIdType.MESH)

    @pl.when(has_right)
    def _():
        pl.semaphore_signal(barrier, inc=1, device_id={"tm": tm + 1},
                            device_id_type=pl.DeviceIdType.MESH)

    pl.semaphore_wait(barrier, has_left.astype(jnp.int32) + has_right.astype(jnp.int32))

    @pl.when(has_right)
    def _():
        for c in up:
            c.start()

    @pl.when(has_left)
    def _():
        for c in down:
            c.start()

    @pl.when(has_left)
    def _():
        for c in up:
            c.wait_recv()
        xl[...] = sxl[...]
        tl[...] = stl[...]

    @pl.when(tm == 0)
    def _():
        xl[...] = jnp.zeros_like(xl)
        tl[...] = jnp.zeros_like(tl)

    @pl.when(has_right)
    def _():
        for c in down:
            c.wait_recv()
        xr[...] = sxr[...]
        tr[...] = str_[...]

    @pl.when(tm == count - 1)
    def _():
        xr[...] = jnp.zeros_like(xr)
        tr[...] = jnp.zeros_like(tr)

    @pl.when(has_right)
    def _():
        for c in up:
            c.wait_send()

    @pl.when(has_left)
    def _():
        for c in down:
            c.wait_send()


def halos(x, te):
    B, T, C = x.shape
    CO = te.shape[2]
    shapes = [(B, HALO, C), (B, HALO, C), (B, 8, CO), (B, 8, CO)]
    return pl.pallas_call(
        halo_kernel,
        out_shape=[jax.ShapeDtypeStruct(s, jnp.float32) for s in shapes],
        in_specs=[pl.BlockSpec(memory_space=pl.ANY)] * 2,
        out_specs=[pl.BlockSpec(memory_space=pltpu.VMEM)] * 4,
        scratch_shapes=[pltpu.VMEM(s, jnp.float32) for s in shapes]
        + [pltpu.SemaphoreType.DMA((4,)), pltpu.SemaphoreType.DMA((4,))],
        compiler_params=pltpu.CompilerParams(
            collective_id=0, has_side_effects=True, vmem_limit_bytes=58 * 2**20),
    )(x, te)


def reduce_kernel(parts, full, near, total, slots, ssend, srecv, send, recv, send2, recv2):
    p = lax.axis_index("weights")
    nb, n = lax.axis_size("batch"), lax.axis_size("batch") * lax.axis_size("tm")
    me = lax.axis_index("tm") * nb + lax.axis_index("batch")
    chunk = full.shape[0] // n

    def place(d):
        r = lax.rem(me + d, n)
        return r, {"tm": r // nb, "batch": lax.rem(r, nb)}

    barrier = pltpu.get_barrier_semaphore()
    pl.semaphore_signal(barrier, inc=1, device_id={"weights": 1 - p},
                        device_id_type=pl.DeviceIdType.MESH)

    @pl.loop(1, n)
    def _(d):
        pl.semaphore_signal(barrier, inc=1, device_id=place(d)[1],
                            device_id_type=pl.DeviceIdType.MESH)

    pl.semaphore_wait(barrier, n)

    def rows(d):
        r = lax.rem(me + d, n)
        return pl.ds(pl.multiple_of(r * chunk, 8), chunk)

    def swap(d):
        return pltpu.make_async_remote_copy(
            src_ref=parts.at[1 - p, rows(d)], dst_ref=near.at[rows(d)],
            send_sem=ssend.at[d - 1], recv_sem=srecv.at[d - 1],
            device_id={"weights": 1 - p}, device_id_type=pl.DeviceIdType.MESH)

    @pl.loop(1, n + 1)
    def _(d):
        swap(d).start()

    def scatter(d):
        r, to = place(d)
        return pltpu.make_async_remote_copy(
            src_ref=total.at[pl.ds(pl.multiple_of(r * chunk, 8), chunk)],
            dst_ref=slots.at[d - 1], send_sem=send.at[d - 1], recv_sem=recv.at[d - 1],
            device_id=to, device_id_type=pl.DeviceIdType.MESH)

    @pl.loop(1, n)
    def _(d):
        swap(d).wait_recv()
        total[rows(d)] = parts[p, rows(d)] + near[rows(d)]
        scatter(d).start()

    own = pl.ds(pl.multiple_of(me * chunk, 8), chunk)
    swap(n).wait_recv()
    full[own] = parts[p, own] + near[own]

    @pl.loop(1, n)
    def _(d):
        scatter(d).wait_recv()
        full[own] += slots[d - 1]

    def gather(d, row):
        return pltpu.make_async_remote_copy(
            src_ref=full.at[own],
            dst_ref=full.at[pl.ds(pl.multiple_of(row * chunk, 8), chunk)],
            send_sem=send2.at[d - 1], recv_sem=recv2.at[d - 1],
            device_id=place(d)[1], device_id_type=pl.DeviceIdType.MESH)

    @pl.loop(1, n)
    def _(d):
        gather(d, me).start()

    @pl.loop(1, n)
    def _(d):
        gather(d, lax.rem(me + n - d, n)).wait_recv()

    @pl.loop(1, n)
    def _(d):
        scatter(d).wait_send()
        gather(d, me).wait_send()

    @pl.loop(1, n + 1)
    def _(d):
        swap(d).wait_send()


def total_panel(parts):
    rows, C = parts.shape[1:]
    n = lax.axis_size("batch") * lax.axis_size("tm")
    f32 = jnp.float32
    dma = pltpu.SemaphoreType.DMA
    return pl.pallas_call(
        reduce_kernel,
        out_shape=jax.ShapeDtypeStruct((rows, C), f32),
        in_specs=[pl.BlockSpec(memory_space=pltpu.VMEM)],
        out_specs=pl.BlockSpec(memory_space=pltpu.VMEM),
        scratch_shapes=[
            pltpu.VMEM((rows, C), f32),
            pltpu.VMEM((rows, C), f32),
            pltpu.VMEM((n - 1, rows // n, C), f32),
            dma((n,)), dma((n,)), dma((n - 1,)), dma((n - 1,)), dma((n - 1,)), dma((n - 1,)),
        ],
        compiler_params=pltpu.CompilerParams(
            collective_id=1, has_side_effects=True, vmem_limit_bytes=24 * 2**20),
    )(parts)


def unpack_kernel(g, conv, conv_b, mix, mix_b, down, down_b, loss):
    C = g.shape[1]
    h = C // 2
    for k in range(TAPS):
        m = k // 2
        conv[k] = g[m * C:(m + 1) * C, (k % 2) * h:(k % 2 + 1) * h]
    mix[:, :h] = g[3 * C:3 * C + h, h:]
    mix[:, h:] = g[3 * C + h:4 * C, h:]
    for k in range(4):
        down[k] = g[(4 + k) * C:(5 + k) * C]
    down_b[...] = g[8 * C:8 * C + 1]
    mix_b[...] = g[8 * C + 1:8 * C + 2, :h]
    conv_b[...] = g[8 * C + 2:8 * C + 3, :h]
    loss[...] = jnp.sum(g[8 * C + 3:8 * C + 4], axis=1, keepdims=True)


def unpack(g):
    C = g.shape[1]
    h = C // 2
    shapes = [(TAPS, C, h), (1, h), (h, C), (1, h), (4, C, C), (1, C), (1, 1)]
    vmem = pl.BlockSpec(memory_space=pltpu.VMEM)
    return pl.pallas_call(
        unpack_kernel,
        out_shape=[jax.ShapeDtypeStruct(s, jnp.float32) for s in shapes],
        in_specs=[vmem],
        out_specs=[vmem] * len(shapes),
        compiler_params=pltpu.CompilerParams(vmem_limit_bytes=16 * 2**20),
    )(g)


def shards(x, te, starts, lengths, wc, bc, wm, bm, wd, bd):
    C, CO = x.shape[2], te.shape[2]
    xl, xr, tl, tr = halos(x, te)
    n = lax.axis_size("batch") * lax.axis_size("tm")
    rows = -(-(8 * C + 8) // (8 * n)) * 8 * n
    parts = local_grads(
        rows, starts, lengths, x, xl, xr, te, tl, tr, wc, bc.reshape(1, C), wm,
        bm.reshape(1, C), wd, bd.reshape(1, CO))
    conv, conv_b, mix, mix_b, down, down_b, loss = unpack(total_panel(parts))
    return (conv, conv_b.reshape(-1), mix, mix_b.reshape(-1), down,
            down_b.reshape(-1), loss.reshape(1))


def solution(mesh):
    clips = P(("groups", "weights", "batch"), "tm", None)
    return jax.shard_map(
        shards,
        mesh=mesh,
        in_specs=(clips, clips, P("groups"), P("groups")) + (P(),) * 6,
        out_specs=(
            P("groups", None, "weights"),
            P(("groups", "weights")),
            P(("groups", "weights"), None),
            P(("groups", "weights")),
            P("groups", None, "weights"),
            P(("groups", "weights")),
            P("groups"),
        ),
        check_vma=False,
    )
```
